256 devices in a mesh: row: 16 (over x_hi, z), col: 16 (over y, x_lo, core).
Axes of the slice: x: 4 (x_hi: 2, x_lo: 2; x = x_hi * 2 + x_lo), y: 4, z: 8, core: 2. Of those that a mesh axis runs over, the one named last changes fastest.
Arguments:
- iterate: float32 [8192, 18432], P('col', 'row'), may hold values from -6 to 6
- inverse: float32 [18432, 18432], P('col', 'row'), may hold values from -0.125 to 0.125
- lower: float32 [], replicated, may hold values from 0.4 to 0.8
Outputs:
- updated: float32 [8192, 18432], P('col', 'row')
The draws below stay inside these ranges and needn't reach their ends.
All inputs are finite; a program needn't handle non-finite values.
Results may differ from the reference program's by a relative error of at most 0.0001.
Values sent between devices are 32-bit elements; how exact they have to be, the bound alone decides.
No kernel may reach another device: no remote copies, remote signals or barrier semaphores. Data moves between devices by JAX's collectives and lax.ppermute only.
A program may use at most 64 MiB of HBM per device.

```python
import jax
import jax.numpy as jnp
from jax import lax

BLOCK = 1152
ROWS_DEV = 512
ORDER = 18432
ROWS = 8192
SPAN = 1152
N_ROW = 16
N_COL = 16


def steps_of(stream_key, shape, cuts, low, high):
    gain = 1.0
    for position, blocks in cuts:
        draws = jax.random.uniform(jax.random.fold_in(jax.random.fold_in(stream_key, 6), position), (blocks,), jnp.float32, low / len(cuts), high / len(cuts))
        gain = gain * jnp.repeat(jnp.exp(draws), shape[position] // blocks).reshape((-1,) + (1,) * (len(shape) - 1 - position))
    return gain


def noise(own_key, dims, scale, most, cuts=(), held_as=jnp.bfloat16):
    loudness = steps_of(own_key, dims, cuts, -0.22, 0.18) if cuts else 1.0
    entries = jax.random.normal(own_key, dims, jnp.float32) * scale * loudness
    return jnp.minimum(jnp.maximum(entries, -most), most).astype(held_as)


def setup_inputs(seed: int = 0) -> dict:
    keys = jax.random.split(jax.random.key(seed), 4)
    iterate = noise(keys[0], (ROWS, ORDER), 1.0, 6.0, ((0, 16), (1, 16)), jnp.float32)
    inverse = noise(keys[1], (ORDER, ORDER), (2 * SPAN) ** -0.5, 0.125, ((0, 16), (1, 16)), jnp.float32)
    lower = jnp.clip(jax.random.uniform(keys[2], (), jnp.float32, 0.4, 0.8), 0.4, 0.8)
    return {"iterate": iterate, "inverse": inverse, "lower": lower}


def coefficients(lower):
    square = lower * lower
    delta = jnp.cbrt(4.0 * (1.0 - square) / (square * square))
    root = jnp.sqrt(1.0 + delta)
    alpha = root + 0.5 * jnp.sqrt(8.0 - 4.0 * delta + 8.0 * (2.0 - square) / (square * root))
    beta = (alpha - 1.0) * (alpha - 1.0) / 4.0
    gamma = alpha + beta - 1.0
    return (beta / gamma, alpha - beta / gamma)

def reference(iterate, inverse, lower):
    keep, lean = coefficients(lower)
    group = BLOCK * (N_ROW // N_COL)
    pieces = []
    for block_row in range(N_COL):
        rows = iterate[block_row * ROWS_DEV:(block_row + 1) * ROWS_DEV]
        total = jnp.zeros((ROWS_DEV, iterate.shape[1]), jnp.float32)
        for section in range(2):
            which = (block_row + section) % N_COL
            total = total + jnp.dot(rows[:, which * group:(which + 1) * group], inverse[which * group:(which + 1) * group], precision=lax.Precision.HIGHEST, preferred_element_type=jnp.float32)
        pieces.append(keep * rows + lean * total)
    return jnp.concatenate(pieces, axis=0)
```

```python
import functools

import jax
import jax.numpy as jnp
import numpy as np
from jax import lax
from jax.experimental import pallas as pl
from jax.experimental.pallas import tpu as pltpu
from jax.sharding import PartitionSpec as P

BOTH = ("row", "col")
SAME = ((0, 0), (0, 2), (0, -2), (1, 1), (1, -1), (1, -3), (0, 4), (1, 3))
OTHER = ((0, 1), (0, -1), (1, 0), (0, 3), (0, -3), (1, -2), (1, 2), (1, 4))
GROUPS = ((0, 3), (3, 5), (5, 8))


def coefficients(lower):
    square = lower * lower
    delta = jnp.cbrt(4.0 * (1.0 - square) / (square * square))
    root = jnp.sqrt(1.0 + delta)
    alpha = root + 0.5 * jnp.sqrt(8.0 - 4.0 * delta + 8.0 * (2.0 - square) / (square * root))
    beta = (alpha - 1.0) * (alpha - 1.0) / 4.0
    gamma = alpha + beta - 1.0
    return (beta / gamma, alpha - beta / gamma)


class Grid:
    def __init__(self, n, ring):
        self.n, self.ring = n, ring

    def device(self, row, col):
        return row * self.n + col % self.n

    def label(self, row, col):
        ring, z = row // self.ring, row % self.ring
        return (ring ^ (col // self.ring), (z - col) % self.ring)

    def row_of(self, label, col):
        return ((col // self.ring) ^ label[0]) * self.ring + (col + label[1]) % self.ring

    def shift(self, by):
        return [
            (r, (r // self.ring) * self.ring + (r % self.ring + by) % self.ring)
            for r in range(self.n)
        ]

    def swap(self):
        return [(r, (r + self.ring) % self.n) for r in range(self.n)]

    def near(self, label, kind, d):
        return (label[0] ^ kind, (label[1] + d) % self.ring)

    def tables(self):
        out = np.zeros((self.n, self.n, 17), np.int32)
        for row in range(self.n):
            for col in range(self.n):
                mine = self.label(row, col)
                out[row, col, 0] = sum(mine) % 2
                kept = OTHER if sum(mine) % 2 else SAME
                theirs = self.label(row, (col + 1) % self.n)
                sent = SAME if sum(theirs) % 2 else OTHER
                for i in range(8):
                    out[row, col, 1 + i] = slot_of(self.near(mine, *kept[i]))
                    out[row, col, 9 + i] = slot_of(self.near(theirs, *sent[i]))
        return out.reshape(self.n * self.n, 17)


def slot_of(label):
    return label[1]


def spread(x, grid):
    size = x.shape[0] // 8
    total = None
    for k in range(8):
        route = []
        for c in range(grid.n):
            route.append((grid.device(c, c), grid.device(grid.row_of((k & 1, k), c), c)))
            route.append((grid.device(c, c - 1), grid.device(grid.row_of(((k & 1) ^ 1, k), c), c)))
        got = lax.ppermute(x[size * k : size * (k + 1)], BOTH, route)
        total = got if total is None else total + got
    return total


def gather(piece, grid):
    up = lambda v: lax.ppermute(v, "row", grid.shift(-1))
    down = lambda v: lax.ppermute(v, "row", grid.shift(1))
    over = lambda v: lax.ppermute(v, "row", grid.swap())
    p = {(0, 0): piece}
    p[0, 1], p[0, -1], p[1, 0] = up(piece), down(piece), over(piece)
    p[0, 2], p[0, -2], p[1, 1] = up(p[0, 1]), down(p[0, -1]), over(p[0, 1])
    p[0, 3], p[0, -3], p[1, -1] = up(p[0, 2]), down(p[0, -2]), over(p[0, -1])
    p[1, 2], p[1, -2] = up(p[1, 1]), down(p[1, -1])
    p[0, 4], p[1, -3] = up(p[0, 3]), down(p[1, -2])
    p[1, 3], p[1, 4] = up(p[1, 2]), down(p[1, -3])
    return p


def product_body(n, flag, *refs):
    size = refs[0].shape[0]
    own, opp, (high, low, kept, sent, a, b) = refs[:n], refs[n : 2 * n], refs[2 * n :]
    t = flag[0]
    for base, group in ((t * (n * size), own), ((1 - t) * (n * size), opp)):
        for i, ref in enumerate(group):
            at = pl.ds(pl.multiple_of(base + i * size, size), size)
            v = ref[...]
            top = v.astype(jnp.bfloat16)
            a[at, :] = top
            b[at, :] = (v - top.astype(jnp.float32)).astype(jnp.bfloat16)
    width = high.shape[1]
    for lo in range(0, width, 256):
        cols = slice(lo, min(lo + 256, width))
        dot = lambda x, y: jnp.dot(x, y, preferred_element_type=jnp.float32)
        r = dot(a[...], high[:, cols]) + (dot(b[...], high[:, cols]) + dot(a[...], low[:, cols]))
        kept[:, cols] = r[: n * size]
        sent[:, cols] = r[n * size :]


def product(flag, own, opp, high, low):
    n = len(own)
    size, depth = own[0].shape
    width = high.shape[1]
    vmem = pl.BlockSpec(memory_space=pltpu.VMEM)
    shape = jax.ShapeDtypeStruct((n * size, width), jnp.float32)
    return pl.pallas_call(
        functools.partial(product_body, n),
        out_shape=(shape, shape),
        in_specs=[pl.BlockSpec(memory_space=pltpu.SMEM)] + [vmem] * (2 * n + 2),
        out_specs=(vmem, vmem),
        scratch_shapes=[pltpu.VMEM((2 * n * size, depth), jnp.bfloat16)] * 2,
        compiler_params=pltpu.CompilerParams(vmem_limit_bytes=24 << 20),
        cost_estimate=pl.CostEstimate(
            flops=2 * 3 * 2 * n * size * depth * width,
            bytes_accessed=2 * n * size * 4 * (depth + width) + 4 * depth * width,
            transcendentals=0,
        ),
    )(flag, *own, *opp, high, low)


def finish_body(table, factors, x, *refs):
    out = refs[-1]
    half = (len(refs) - 1) // 2
    kept, sent = refs[:half], refs[half:-1]
    keep, lean = factors[0], factors[1]
    size = x.shape[0] // 8
    i = 0
    for ref in kept:
        for lo in range(0, ref.shape[0], size):
            at = pl.ds(pl.multiple_of(table[1 + i] * size, size), size)
            out[at, :] = keep * x[at, :] + lean * ref[lo : lo + size, :]
            i += 1
    i = 0
    for ref in sent:
        for lo in range(0, ref.shape[0], size):
            at = pl.ds(pl.multiple_of(table[9 + i] * size, size), size)
            out[at, :] = out[at, :] + lean * ref[lo : lo + size, :]
            i += 1


def finish(table, factors, x, kept, sent):
    vmem = pl.BlockSpec(memory_space=pltpu.VMEM)
    smem = pl.BlockSpec(memory_space=pltpu.SMEM)
    return pl.pallas_call(
        finish_body,
        out_shape=jax.ShapeDtypeStruct(x.shape, jnp.float32),
        in_specs=[smem, smem] + [vmem] * (1 + len(kept) + len(sent)),
        out_specs=vmem,
        compiler_params=pltpu.CompilerParams(vmem_limit_bytes=24 << 20),
        cost_estimate=pl.CostEstimate(
            flops=5 * x.size, bytes_accessed=16 * x.size, transcendentals=0
        ),
    )(table, factors, x, *kept, *sent)


def shards(grid, iterate, inverse, lower):
    here = lax.axis_index("row") * grid.n + lax.axis_index("col")
    table = lax.dynamic_index_in_dim(jnp.asarray(grid.tables()), here, 0, keepdims=False)
    factors = jnp.stack(coefficients(lower))
    pieces = gather(spread(iterate, grid), grid)
    high = inverse.astype(jnp.bfloat16)
    low = (inverse - lax.reduce_precision(inverse, 8, 7)).astype(jnp.bfloat16)
    back = [((c + 1) % grid.n, c) for c in range(grid.n)]
    kept, sent = [], []
    for lo, hi in GROUPS:
        own, opp = [pieces[k] for k in SAME[lo:hi]], [pieces[k] for k in OTHER[lo:hi]]
        stay, go = product(table, own, opp, high, low)
        kept.append(stay)
        sent.append(lax.ppermute(go, "col", back))
    return finish(table, factors, iterate, kept, sent)


def solution(mesh):
    grid = Grid(mesh.shape["row"], mesh.shape["row"] // 2)
    placed = (P("col", "row"), P("col", "row"), P())
    return jax.shard_map(
        functools.partial(shards, grid),
        mesh=mesh,
        in_specs=placed,
        out_specs=P("col", "row"),
        check_vma=False,
    )
```

```python
import functools

import jax
import jax.numpy as jnp
import numpy as np
from jax import lax
from jax.experimental import pallas as pl
from jax.experimental.pallas import tpu as pltpu
from jax.sharding import PartitionSpec as P

BOTH = ("row", "col")
SAME = ((0, 0), (0, 2), (0, -2), (1, 1), (1, -1), (1, -3), (0, 4), (1, 3))
OTHER = ((0, 1), (0, -1), (1, 0), (0, 3), (0, -3), (1, -2), (1, 2), (1, 4))
GROUPS = ((0, 1), (1, 3), (3, 5), (5, 7), (7, 8))
PLAN = {
    (0, 0): (((2, 0), (0, 1)), (((0, 2), (0, 0), (0, 4), (1, 5)), ((0, 6), (1, 1)), ((1, 3), (1, 7)))),
    (0, 1): (((0, 3), (1, 0)), (((0, 0), (1, 5), (1, 1), (0, 4)), ((1, 3), (1, 7)), ((0, 6), (0, 2)))),
    (1, 0): (((2, 0), (0, 1)), (((0, 7), (1, 6), (1, 4), (0, 3)), ((0, 5), (1, 2)), ((1, 0), (0, 1)))),
    (1, 1): (((3, 0), (0, 1)), (((1, 4), (1, 2), (0, 7), (0, 3)), ((0, 1), (1, 6)), ((0, 5), (1, 0)))),
}


def coefficients(lower):
    square = lower * lower
    delta = jnp.cbrt(4.0 * (1.0 - square) / (square * square))
    root = jnp.sqrt(1.0 + delta)
    alpha = root + 0.5 * jnp.sqrt(8.0 - 4.0 * delta + 8.0 * (2.0 - square) / (square * root))
    beta = (alpha - 1.0) * (alpha - 1.0) / 4.0
    gamma = alpha + beta - 1.0
    return (beta / gamma, alpha - beta / gamma)


class Grid:
    def __init__(self, n, ring):
        self.n, self.ring = n, ring

    def device(self, row, col):
        return row * self.n + col % self.n

    def label(self, row, col):
        ring, z = row // self.ring, row % self.ring
        return (ring ^ (col // self.ring), (z - col) % self.ring)

    def row_of(self, label, col):
        return ((col // self.ring) ^ label[0]) * self.ring + (col + label[1]) % self.ring

    def shift(self, by):
        return [
            (r, (r // self.ring) * self.ring + (r % self.ring + by) % self.ring)
            for r in range(self.n)
        ]

    def moved(self, row, col, move):
        x = (row // self.ring * 2 + col // 2 % 2 + move[0]) % 4
        y = (col // 4 + move[1]) % 4
        return (x // 2 * self.ring + row % self.ring, y * 4 + x % 2 * 2 + col % 2)

    def senders(self, block, c):
        root = (c, (c - block) % self.n)
        return [root] + [self.moved(*root, m) for m in PLAN[block, c % 2][0]]

    def swap(self):
        return [(r, (r + self.ring) % self.n) for r in range(self.n)]

    def near(self, label, kind, d):
        return (label[0] ^ kind, (label[1] + d) % self.ring)

    def tables(self):
        out = np.zeros((self.n, self.n, 17), np.int32)
        for row in range(self.n):
            for col in range(self.n):
                mine = self.label(row, col)
                out[row, col, 0] = sum(mine) % 2
                kept = OTHER if sum(mine) % 2 else SAME
                theirs = self.label(row, (col + 1) % self.n)
                sent = SAME if sum(theirs) % 2 else OTHER
                for i in range(8):
                    out[row, col, 1 + i] = slot_of(0, col, self.near(mine, *kept[i]))
                    out[row, col, 9 + i] = slot_of(1, col + 1, self.near(theirs, *sent[i]))
        return out.reshape(self.n * self.n, 17)


def slot_of(block, c, label):
    return [h for holders in PLAN[block, c % 2][1] for h in holders].index(label)


def spread(x, grid):
    size = x.shape[0] // 8
    groups = [(c, b) for c in range(grid.n) for b in range(2)]

    def hop(relay):
        return [
            (grid.device(*grid.senders(b, c)[0]), grid.device(*grid.senders(b, c)[relay]))
            for c, b in groups
        ]

    def deal(who, j):
        return [
            (
                grid.device(*grid.senders(b, c)[s]),
                grid.device(grid.row_of(PLAN[b, c % 2][1][s][j], c), c),
            )
            for c, b in groups
            for s in who
        ]

    held = [lax.ppermute(x[4 * size : 6 * size], BOTH, hop(1)), lax.ppermute(x[6 * size :], BOTH, hop(2))]
    got = [lax.ppermute(x[size * j : size * (j + 1)], BOTH, deal((0,), j)) for j in range(4)]
    both = [held[0][size * j : size * (j + 1)] + held[1][size * j : size * (j + 1)] for j in range(2)]
    got += [lax.ppermute(both[j], BOTH, deal((1, 2), j)) for j in range(2)]
    return functools.reduce(jnp.add, got), both


def after(value, *others):
    return lax.optimization_barrier((value, *others))[0]


def stages(piece, grid, work, back):
    def move(v, route, where, others):
        with jax.named_scope("piece_%d_%d" % where):
            return lax.ppermute(after(v, *others) if others else v, "row", route)

    up = lambda v, where, *o: move(v, grid.shift(-1), where, o)
    down = lambda v, where, *o: move(v, grid.shift(1), where, o)
    over = lambda v, where, *o: move(v, grid.swap(), where, o)
    p = {(0, 0): piece}

    def far(d, *o):
        p[0, d] = (up if d > 0 else down)(p[0, d - 1 if d > 0 else d + 1], (0, d), *o)

    def cross(d, *o):
        p[1, d] = over(p[0, d], (1, d), *o)

    def along(d, *o):
        p[1, d] = (up if 0 < d < 4 else down)(p[1, d - 1 if 0 < d < 4 else (d + 1 if d < 0 else -3)], (1, d), *o)

    far(1), far(-1), cross(0)
    far(2), far(-2), cross(1)
    far(3), far(-3), cross(-1)
    along(2), along(-2)
    far(4), along(-3)
    along(3), along(4)
    for i in range(5):
        back(i, work(i, p))


def product_body(n, flag, *refs):
    size = refs[0].shape[0]
    own, opp, (high, low, kept, sent, f, a, b, arrive, leave) = refs[:n], refs[n : 2 * n], refs[2 * n :]
    t = flag[0]
    loads = []
    for base, group in ((t * (n * size), own), ((1 - t) * (n * size), opp)):
        for i, ref in enumerate(group):
            at = pl.ds(pl.multiple_of(base + i * size, size), size)
            loads.append(pltpu.make_async_copy(ref, f.at[at], arrive.at[len(loads)]))
    for load in loads:
        load.start()
    for load in loads:
        load.wait()
    for lo in range(0, 2 * n * size, size):
        rows = slice(lo, lo + size)
        v = f[rows, :]
        top = v.astype(jnp.bfloat16)
        a[rows, :] = top
        b[rows, :] = (v - top.astype(jnp.float32)).astype(jnp.bfloat16)
    width = high.shape[1]
    for lo in range(0, width, 256):
        cols = slice(lo, min(lo + 256, width))
        dot = lambda x, y: jnp.dot(x, y, preferred_element_type=jnp.float32)
        f[:, cols] = dot(a[...], high[:, cols]) + (dot(b[...], high[:, cols]) + dot(a[...], low[:, cols]))
    stores = [
        pltpu.make_async_copy(f.at[pl.ds(n * size, n * size)], sent, leave.at[0]),
        pltpu.make_async_copy(f.at[pl.ds(0, n * size)], kept, leave.at[1]),
    ]
    for store in stores:
        store.start()
    for store in stores:
        store.wait()


def product(flag, own, opp, high, low):
    n = len(own)
    size, depth = own[0].shape
    width = high.shape[1]
    vmem = pl.BlockSpec(memory_space=pltpu.VMEM)
    free = pl.BlockSpec(memory_space=pl.ANY)
    shape = jax.ShapeDtypeStruct((n * size, width), jnp.float32)
    return pl.pallas_call(
        functools.partial(product_body, n),
        out_shape=(shape, shape),
        in_specs=[pl.BlockSpec(memory_space=pltpu.SMEM)] + [free] * (2 * n) + [vmem] * 2,
        out_specs=(free, free),
        scratch_shapes=[
            pltpu.VMEM((2 * n * size, depth), jnp.float32),
            pltpu.VMEM((2 * n * size, depth), jnp.bfloat16),
            pltpu.VMEM((2 * n * size, depth), jnp.bfloat16),
            pltpu.SemaphoreType.DMA((2 * n,)),
            pltpu.SemaphoreType.DMA((2,)),
        ],
        compiler_params=pltpu.CompilerParams(vmem_limit_bytes=14 << 20),
        cost_estimate=pl.CostEstimate(
            flops=2 * 3 * 2 * n * size * depth * width,
            bytes_accessed=2 * n * size * 4 * (depth + width) + 4 * depth * width,
            transcendentals=0,
        ),
    )(flag, *own, *opp, high, low)


def finish_body(n, table, factors, x, *refs):
    parts, (out, f, g, arrive, leave) = refs[:-5], refs[-5:]
    keep, lean = factors[0], factors[1]
    size = x.shape[0] // 8
    loads, lo = [pltpu.make_async_copy(x, f, arrive.at[0])], 0
    for ref in parts:
        rows = ref.shape[0]
        loads.append(pltpu.make_async_copy(ref, g.at[pl.ds(lo, rows)], arrive.at[len(loads)]))
        lo += rows
    for load in loads:
        load.start()
    for load in loads:
        load.wait()
    for i in range(n):
        at = pl.ds(pl.multiple_of(table[1 + i] * size, size), size)
        held = keep * f[at, :] if i < 8 else f[at, :]
        f[at, :] = held + lean * g[i * size : (i + 1) * size, :]
    store = pltpu.make_async_copy(f, out, leave.at[0])
    store.start()
    store.wait()


def finish(table, factors, x, parts):
    free = pl.BlockSpec(memory_space=pl.ANY)
    smem = pl.BlockSpec(memory_space=pltpu.SMEM)
    rows = sum(p.shape[0] for p in parts)
    return pl.pallas_call(
        functools.partial(finish_body, rows * 8 // x.shape[0]),
        out_shape=jax.ShapeDtypeStruct(x.shape, jnp.float32),
        in_specs=[smem, smem] + [free] * (1 + len(parts)),
        out_specs=free,
        scratch_shapes=[
            pltpu.VMEM(x.shape, jnp.float32),
            pltpu.VMEM((rows, x.shape[1]), jnp.float32),
            pltpu.SemaphoreType.DMA((1 + len(parts),)),
            pltpu.SemaphoreType.DMA((1,)),
        ],
        compiler_params=pltpu.CompilerParams(vmem_limit_bytes=14 << 20),
        cost_estimate=pl.CostEstimate(
            flops=3 * rows * x.shape[1], bytes_accessed=12 * rows * x.shape[1], transcendentals=0
        ),
    )(table, factors, x, *parts)


def last_body(first, table, factors, held, *refs):
    parts, (out, f, arrive, leave) = refs[:-4], refs[-4:]
    size = held.shape[0] // 8
    n = f.shape[0] // size
    at = [pl.ds(pl.multiple_of(table[9 + first + i] * size, size), size) for i in range(n)]
    mine = [pl.ds(i * size, size) for i in range(n)]
    loads = [pltpu.make_async_copy(held.at[at[i]], f.at[mine[i]], arrive.at[i]) for i in range(n)]
    stores = [pltpu.make_async_copy(f.at[mine[i]], out.at[at[i]], leave.at[i]) for i in range(n)]
    for load in loads:
        load.start()
    i = 0
    for part in parts:
        for lo in range(0, part.shape[0], size):
            loads[i].wait()
            f[mine[i], :] = f[mine[i], :] + factors[1] * part[lo : lo + size, :]
            stores[i].start()
            i += 1
    for store in stores:
        store.wait()


def last(first, table, factors, held, parts):
    free = pl.BlockSpec(memory_space=pl.ANY)
    smem = pl.BlockSpec(memory_space=pltpu.SMEM)
    vmem = pl.BlockSpec(memory_space=pltpu.VMEM)
    n = 8 - first
    return pl.pallas_call(
        functools.partial(last_body, first),
        out_shape=jax.ShapeDtypeStruct(held.shape, jnp.float32),
        in_specs=[smem, smem, free] + [vmem] * len(parts),
        out_specs=free,
        input_output_aliases={2: 0},
        scratch_shapes=[
            pltpu.VMEM((held.shape[0] // 8 * n, held.shape[1]), jnp.float32),
            pltpu.SemaphoreType.DMA((n,)),
            pltpu.SemaphoreType.DMA((n,)),
        ],
        compiler_params=pltpu.CompilerParams(vmem_limit_bytes=6 << 20),
    )(table, factors, held, *parts)


def shards(grid, iterate, inverse, lower):
    here = lax.axis_index("row") * grid.n + lax.axis_index("col")
    table = lax.dynamic_index_in_dim(jnp.asarray(grid.tables()), here, 0, keepdims=False)
    factors = jnp.stack(coefficients(lower))
    piece, relayed = spread(iterate, grid)
    inverse = after(inverse, *relayed)
    high = inverse.astype(jnp.bfloat16)
    low = (inverse - lax.reduce_precision(inverse, 8, 7)).astype(jnp.bfloat16)
    piece, high, low, table, factors = lax.optimization_barrier((piece, high, low, table, factors))
    back = [((c + 1) % grid.n, c) for c in range(grid.n)]
    kept, sent = [], []

    def work(i, pieces, *others):
        lo, hi = GROUPS[i]
        own, opp = [pieces[k] for k in SAME[lo:hi]], [pieces[k] for k in OTHER[lo:hi]]
        if others:
            own[0] = after(own[0], *(pieces[k] for k in others))
        if i >= 2:
            own[0], sent[i - 2] = lax.optimization_barrier((own[0], sent[i - 2]))
        stay, go = product(table, own, opp, high, low)
        kept.append(stay)
        return go

    def send(i, go):
        with jax.named_scope("return_%d" % i):
            sent.append(lax.ppermute(go, "col", back))

    stages(piece, grid, work, send)
    early = 3
    out = finish(table, factors, iterate, kept + sent[:early])
    return last(GROUPS[early][0], table, factors, out, sent[early:])


def solution(mesh):
    grid = Grid(mesh.shape["row"], mesh.shape["row"] // 2)
    placed = (P("col", "row"), P("col", "row"), P())
    return jax.shard_map(
        functools.partial(shards, grid),
        mesh=mesh,
        in_specs=placed,
        out_specs=P("col", "row"),
        check_vma=False,
    )
```

```python
import functools

import jax
import jax.numpy as jnp
import numpy as np
from jax import lax
from jax.experimental import pallas as pl
from jax.experimental.pallas import tpu as pltpu
from jax.sharding import PartitionSpec as P

BOTH = ("row", "col")
SAME = ((0, 0), (0, 2), (0, -2), (1, 1), (1, -1), (1, -3), (0, 4), (1, 3))
OTHER = ((0, 1), (0, -1), (1, 0), (0, 3), (0, -3), (1, -2), (1, 2), (1, 4))
GROUPS = ((0, 1), (1, 3), (3, 5), (5, 7), (7, 8))
PLAN = {
    (0, 0): (((2, 0), (0, 1)), (((0, 0), (1, 5), (0, 4), (0, 2)), ((1, 1), (0, 6)), ((1, 3), (1, 7)))),
    (0, 1): (((0, 3), (1, 0)), (((0, 0), (0, 4), (1, 1), (1, 5)), ((1, 7), (1, 3)), ((0, 6), (0, 2)))),
    (1, 0): (((2, 0), (0, 1)), (((0, 7), (0, 3), (1, 4), (1, 6)), ((1, 2), (0, 5)), ((1, 0), (0, 1)))),
    (1, 1): (((3, 0), (0, 1)), (((0, 7), (1, 2), (1, 4), (0, 3)), ((0, 1), (1, 6)), ((0, 5), (1, 0)))),
}


def coefficients(lower):
    square = lower * lower
    delta = jnp.cbrt(4.0 * (1.0 - square) / (square * square))
    root = jnp.sqrt(1.0 + delta)
    alpha = root + 0.5 * jnp.sqrt(8.0 - 4.0 * delta + 8.0 * (2.0 - square) / (square * root))
    beta = (alpha - 1.0) * (alpha - 1.0) / 4.0
    gamma = alpha + beta - 1.0
    return (beta / gamma, alpha - beta / gamma)


class Grid:
    def __init__(self, n, ring):
        self.n, self.ring = n, ring

    def device(self, row, col):
        return row * self.n + col % self.n

    def label(self, row, col):
        ring, z = row // self.ring, row % self.ring
        return (ring ^ (col // self.ring), (z - col) % self.ring)

    def row_of(self, label, col):
        return ((col // self.ring) ^ label[0]) * self.ring + (col + label[1]) % self.ring

    def shift(self, by):
        return [
            (r, (r // self.ring) * self.ring + (r % self.ring + by) % self.ring)
            for r in range(self.n)
        ]

    def moved(self, row, col, move):
        x = (row // self.ring * 2 + col // 2 % 2 + move[0]) % 4
        y = (col // 4 + move[1]) % 4
        return (x // 2 * self.ring + row % self.ring, y * 4 + x % 2 * 2 + col % 2)

    def senders(self, block, c):
        root = (c, (c - block) % self.n)
        return [root] + [self.moved(*root, m) for m in PLAN[block, c % 2][0]]

    def swap(self):
        return [(r, (r + self.ring) % self.n) for r in range(self.n)]

    def near(self, label, kind, d):
        return (label[0] ^ kind, (label[1] + d) % self.ring)

    def tables(self):
        out = np.zeros((self.n, self.n, 18), np.int32)
        for row in range(self.n):
            for col in range(self.n):
                mine = self.label(row, col)
                out[row, col, 0] = sum(mine) % 2
                kept = OTHER if sum(mine) % 2 else SAME
                at = slot_of(sum(mine) % 2, col, mine)
                out[row, col, 17] = at if at < 4 else 4 + at % 2
                theirs = self.label(row, (col + 1) % self.n)
                sent = SAME if sum(theirs) % 2 else OTHER
                for i in range(8):
                    out[row, col, 1 + i] = slot_of(0, col, self.near(mine, *kept[i]))
                    out[row, col, 9 + i] = slot_of(1, col + 1, self.near(theirs, *sent[i]))
        return out.reshape(self.n * self.n, 18)


def slot_of(block, c, label):
    return [h for holders in PLAN[block, c % 2][1] for h in holders].index(label)


def cut_body(starts, x, *refs):
    outs, leave = refs[:-1], refs[-1]
    copies = [
        pltpu.make_async_copy(x.at[pl.ds(at, out.shape[0])], out, leave.at[i])
        for i, (at, out) in enumerate(zip(starts, outs))
    ]
    for copy in copies:
        copy.start()
    for copy in copies:
        copy.wait()


def cut(x, eighths):
    size, free = x.shape[0] // 8, pl.BlockSpec(memory_space=pl.ANY)
    return pl.pallas_call(
        functools.partial(cut_body, [size * sum(eighths[:i]) for i in range(len(eighths))]),
        out_shape=tuple(jax.ShapeDtypeStruct((size * n, x.shape[1]), x.dtype) for n in eighths),
        in_specs=[pl.BlockSpec(memory_space=pltpu.HBM)],
        out_specs=(free,) * len(eighths),
        scratch_shapes=[pltpu.SemaphoreType.DMA((len(eighths),))],
        compiler_params=pltpu.CompilerParams(vmem_limit_bytes=1 << 20),
        cost_estimate=pl.CostEstimate(flops=0, bytes_accessed=8 * x.size, transcendentals=0),
    )(x)


def pick_body(table, *refs):
    *parts, out, arrive = refs
    for i, part in enumerate(parts):

        @pl.when(table[17] == i)
        def _():
            copy = pltpu.make_async_copy(part, out, arrive)
            copy.start()
            copy.wait()


def pick(table, parts):
    free = pl.BlockSpec(memory_space=pl.ANY)
    return pl.pallas_call(
        pick_body,
        out_shape=jax.ShapeDtypeStruct(parts[0].shape, parts[0].dtype),
        in_specs=[pl.BlockSpec(memory_space=pltpu.SMEM)] + [free] * len(parts),
        out_specs=free,
        scratch_shapes=[pltpu.SemaphoreType.DMA],
        compiler_params=pltpu.CompilerParams(vmem_limit_bytes=1 << 20),
    )(table, *parts)


def spread(x, table, grid):
    size = x.shape[0] // 8
    groups = [(c, b) for c in range(grid.n) for b in range(2)]

    def hop(relay):
        return [
            (grid.device(*grid.senders(b, c)[0]), grid.device(*grid.senders(b, c)[relay]))
            for c, b in groups
        ]

    def deal(who, j):
        return [
            (
                grid.device(*grid.senders(b, c)[s]),
                grid.device(grid.row_of(PLAN[b, c % 2][1][s][j], c), c),
            )
            for c, b in groups
            for s in who
        ]

    *eighths, third, fourth = cut(x, (1, 1, 1, 1, 2, 2))
    held = [lax.ppermute(third, BOTH, hop(1)), lax.ppermute(fourth, BOTH, hop(2))]
    got = [lax.ppermute(eighths[j], BOTH, deal((0,), j)) for j in range(4)]
    both = [held[0][size * j : size * (j + 1)] + held[1][size * j : size * (j + 1)] for j in range(2)]
    got += [lax.ppermute(both[j], BOTH, deal((1, 2), j)) for j in range(2)]
    return pick(table, got), both


def after(value, *others):
    return lax.optimization_barrier((value, *others))[0]


def stages(piece, grid, work, back):
    def move(v, route, where, others):
        with jax.named_scope("piece_%d_%d" % where):
            return lax.ppermute(after(v, *others) if others else v, "row", route)

    up = lambda v, where, *o: move(v, grid.shift(-1), where, o)
    down = lambda v, where, *o: move(v, grid.shift(1), where, o)
    over = lambda v, where, *o: move(v, grid.swap(), where, o)
    p = {(0, 0): piece}

    def far(d, *o):
        p[0, d] = (up if d > 0 else down)(p[0, d - 1 if d > 0 else d + 1], (0, d), *o)

    def cross(d, *o):
        p[1, d] = over(p[0, d], (1, d), *o)

    def along(d, *o):
        p[1, d] = (up if 0 < d < 4 else down)(p[1, d - 1 if 0 < d < 4 else (d + 1 if d < 0 else -3)], (1, d), *o)

    far(1), far(-1), cross(0)
    far(2), far(-2), cross(1)
    far(3), far(-3), cross(-1)
    along(2), along(-2)
    far(4), along(-3)
    along(3), along(4)
    for i in range(5):
        back(i, work(i, p))


def product_body(n, flag, *refs):
    size = refs[0].shape[0]
    own, opp, (high, low, kept, sent, f, a, b, arrive, leave) = refs[:n], refs[n : 2 * n], refs[2 * n :]
    t = flag[0]
    loads = []
    for base, group in ((t * (n * size), own), ((1 - t) * (n * size), opp)):
        for i, ref in enumerate(group):
            at = pl.ds(pl.multiple_of(base + i * size, size), size)
            loads.append(pltpu.make_async_copy(ref, f.at[at], arrive.at[len(loads)]))
    for load in loads:
        load.start()
    for load in loads:
        load.wait()
    for lo in range(0, 2 * n * size, size):
        rows = slice(lo, lo + size)
        v = f[rows, :]
        top = v.astype(jnp.bfloat16)
        a[rows, :] = top
        b[rows, :] = (v - top.astype(jnp.float32)).astype(jnp.bfloat16)
    width = high.shape[1]
    for lo in range(0, width, 256):
        cols = slice(lo, min(lo + 256, width))
        dot = lambda x, y: jnp.dot(x, y, preferred_element_type=jnp.float32)
        f[:, cols] = dot(a[...], high[:, cols]) + (dot(b[...], high[:, cols]) + dot(a[...], low[:, cols]))
    stores = [
        pltpu.make_async_copy(f.at[pl.ds(n * size, n * size)], sent, leave.at[0]),
        pltpu.make_async_copy(f.at[pl.ds(0, n * size)], kept, leave.at[1]),
    ]
    for store in stores:
        store.start()
    for store in stores:
        store.wait()


def product(flag, own, opp, high, low):
    n = len(own)
    size, depth = own[0].shape
    width = high.shape[1]
    vmem = pl.BlockSpec(memory_space=pltpu.VMEM)
    free = pl.BlockSpec(memory_space=pl.ANY)
    shape = jax.ShapeDtypeStruct((n * size, width), jnp.float32)
    return pl.pallas_call(
        functools.partial(product_body, n),
        out_shape=(shape, shape),
        in_specs=[pl.BlockSpec(memory_space=pltpu.SMEM)] + [free] * (2 * n) + [vmem] * 2,
        out_specs=(free, free),
        scratch_shapes=[
            pltpu.VMEM((2 * n * size, depth), jnp.float32),
            pltpu.VMEM((2 * n * size, depth), jnp.bfloat16),
            pltpu.VMEM((2 * n * size, depth), jnp.bfloat16),
            pltpu.SemaphoreType.DMA((2 * n,)),
            pltpu.SemaphoreType.DMA((2,)),
        ],
        compiler_params=pltpu.CompilerParams(vmem_limit_bytes=14 << 20),
        cost_estimate=pl.CostEstimate(
            flops=2 * 3 * 2 * n * size * depth * width,
            bytes_accessed=2 * n * size * 4 * (depth + width) + 4 * depth * width,
            transcendentals=0,
        ),
    )(flag, *own, *opp, high, low)


def finish_body(n, table, factors, x, *refs):
    parts, (out, g, arrive) = refs[:-3], refs[-3:]
    keep, lean = factors[0], factors[1]
    size = x.shape[0] // 8
    loads, lo = [pltpu.make_async_copy(x, out, arrive.at[0])], 0
    for ref in parts:
        rows = ref.shape[0]
        loads.append(pltpu.make_async_copy(ref, g.at[pl.ds(lo, rows)], arrive.at[len(loads)]))
        lo += rows
    for load in loads:
        load.start()
    for load in loads:
        load.wait()
    for i in range(n):
        at = pl.ds(pl.multiple_of(table[1 + i] * size, size), size)
        held = keep * out[at, :] if i < 8 else out[at, :]
        out[at, :] = held + lean * g[i * size : (i + 1) * size, :]


def finish(table, factors, x, parts):
    free = pl.BlockSpec(memory_space=pl.ANY)
    smem = pl.BlockSpec(memory_space=pltpu.SMEM)
    rows = sum(p.shape[0] for p in parts)
    return pl.pallas_call(
        functools.partial(finish_body, rows * 8 // x.shape[0]),
        out_shape=jax.ShapeDtypeStruct(x.shape, jnp.float32),
        in_specs=[smem, smem] + [free] * (1 + len(parts)),
        out_specs=pl.BlockSpec(memory_space=pltpu.VMEM),
        scratch_shapes=[
            pltpu.VMEM((rows, x.shape[1]), jnp.float32),
            pltpu.SemaphoreType.DMA((1 + len(parts),)),
        ],
        compiler_params=pltpu.CompilerParams(vmem_limit_bytes=14 << 20),
        cost_estimate=pl.CostEstimate(
            flops=3 * rows * x.shape[1], bytes_accessed=12 * rows * x.shape[1], transcendentals=0
        ),
    )(table, factors, x, *parts)


def last_body(first, table, factors, held, *refs):
    parts, (out, f, leave) = refs[:-3], refs[-3:]
    size = held.shape[0] // 8
    at = [pl.ds(pl.multiple_of(table[9 + i] * size, size), size) for i in range(8)]
    mine = [pl.ds(i * size, size) for i in range(8 - first)]
    stores = [pltpu.make_async_copy(held.at[at[i]], out.at[at[i]], leave.at[i]) for i in range(first)]
    for store in stores:
        store.start()
    i = 0
    for part in parts:
        for lo in range(0, part.shape[0], size):
            f[mine[i], :] = held[at[first + i], :] + factors[1] * part[lo : lo + size, :]
            stores.append(pltpu.make_async_copy(f.at[mine[i]], out.at[at[first + i]], leave.at[first + i]))
            stores[-1].start()
            i += 1
    for store in stores:
        store.wait()


def last(first, table, factors, held, parts):
    free = pl.BlockSpec(memory_space=pl.ANY)
    smem = pl.BlockSpec(memory_space=pltpu.SMEM)
    vmem = pl.BlockSpec(memory_space=pltpu.VMEM)
    return pl.pallas_call(
        functools.partial(last_body, first),
        out_shape=jax.ShapeDtypeStruct(held.shape, jnp.float32),
        in_specs=[smem, smem, vmem] + [vmem] * len(parts),
        out_specs=free,
        scratch_shapes=[
            pltpu.VMEM((held.shape[0] // 8 * (8 - first), held.shape[1]), jnp.float32),
            pltpu.SemaphoreType.DMA((8,)),
        ],
        compiler_params=pltpu.CompilerParams(vmem_limit_bytes=6 << 20),
    )(table, factors, held, *parts)


def shards(grid, iterate, inverse, lower):
    here = lax.axis_index("row") * grid.n + lax.axis_index("col")
    table = lax.dynamic_index_in_dim(jnp.asarray(grid.tables()), here, 0, keepdims=False)
    factors = jnp.stack(coefficients(lower))
    piece, relayed = spread(iterate, table, grid)
    inverse = after(inverse, *relayed)
    high = inverse.astype(jnp.bfloat16)
    low = (inverse - lax.reduce_precision(inverse, 8, 7)).astype(jnp.bfloat16)
    piece, high, low, table, factors = lax.optimization_barrier((piece, high, low, table, factors))
    back = [((c + 1) % grid.n, c) for c in range(grid.n)]
    kept, sent = [], []

    def work(i, pieces, *others):
        lo, hi = GROUPS[i]
        own, opp = [pieces[k] for k in SAME[lo:hi]], [pieces[k] for k in OTHER[lo:hi]]
        if others:
            own[0] = after(own[0], *(pieces[k] for k in others))
        if i >= 2:
            own[0], sent[i - 2] = lax.optimization_barrier((own[0], sent[i - 2]))
        stay, go = product(table, own, opp, high, low)
        kept.append(stay)
        return go

    def send(i, go):
        with jax.named_scope("return_%d" % i):
            sent.append(lax.ppermute(go, "col", back))

    stages(piece, grid, work, send)
    early = 3
    out = finish(table, factors, iterate, kept + sent[:early])
    return last(GROUPS[early][0], table, factors, out, sent[early:])


def solution(mesh):
    grid = Grid(mesh.shape["row"], mesh.shape["row"] // 2)
    placed = (P("col", "row"), P("col", "row"), P())
    return jax.shard_map(
        functools.partial(shards, grid),
        mesh=mesh,
        in_specs=placed,
        out_specs=P("col", "row"),
        check_vma=False,
    )
```
